32 devices in a mesh: section: 4 (over x, core), ctx: 2 (over y), tp: 4 (over z).
Axes of the slice: x: 2, y: 2, z: 4, core: 2. Of those that a mesh axis runs over, the one named last changes fastest.
Arguments:
- stretch_order: int32 [2, 2], replicated, may hold values from 0 to 3, as said below
- queries: bfloat16 [4, 1024, 2048], P('section', 'ctx', 'tp'), may hold values from -60 to 60
- key_rows: bfloat16 [4, 1024, 512], P('section', 'ctx', 'tp'), may hold values from -7 to 7
- value_rows: bfloat16 [4, 1024, 512], P('section', 'ctx', 'tp'), may hold values from -5 to 5
- out_grad: bfloat16 [4, 1024, 4096], P('section', ('ctx', 'tp')), may hold values from -6 to 6
- query_weight: bfloat16 [4, 4096, 2048], P('section', None, 'tp'), may hold values from -0.09375 to 0.09375
- key_weight: bfloat16 [4, 4096, 512], P('section', None, 'tp'), may hold values from -0.09375 to 0.09375
- value_weight: bfloat16 [4, 4096, 512], P('section', None, 'tp'), may hold values from -0.09375 to 0.09375
- output_weight: bfloat16 [4, 2048, 4096], P('section', 'tp'), may hold values from -0.125 to 0.125
Outputs:
- sent_grad: bfloat16 [4, 1024, 4096], P('section', ('ctx', 'tp'))
- key_grad: bfloat16 [4, 1024, 512], P('section', 'ctx', 'tp')
- value_grad: bfloat16 [4, 1024, 512], P('section', 'ctx', 'tp')
The draws below stay inside these ranges and needn't reach their ends.
Inputs may be any that keep to these rules, and one draw needn't show every extreme that they name: `stretch_order`: row c lists the ids of the two blocks of 256 consecutive positions stored, in that order, at ctx index c; the two ids of a row sum to 3 and every id occurs once.
All inputs are finite; a program needn't handle non-finite values.
Results may differ from the reference program's by a relative error of at most 0.015.
Values may be sent and summed in bfloat16 or wider, within the bound.
A program may use at most 128 MiB of HBM per device.

```python
import jax
import jax.numpy as jnp
from jax import lax

D = 4096
HD = 128
HQ = 16
KV = 4
TOK_DEV = 512
TOKENS = 1024
SECTIONS = 4
N_CTX = 2
N_TP = 4


def draw_stretch_order(key, part):
    key_perm, key_flip = jax.random.split(jax.random.fold_in(key, 77))
    first = jax.random.permutation(key_perm, N_CTX).astype(jnp.int32)
    second = (2 * N_CTX - 1 - first).astype(jnp.int32)
    flip = jax.random.randint(key_flip, (N_CTX,), 0, 2)
    left = jnp.where(flip == 1, second, first)
    right = jnp.where(flip == 1, first, second)
    return jnp.stack([left, right], axis=1).astype(jnp.int32)


def query_key_pair(key):
    base = jax.random.fold_in(key, 4242)
    key_q, key_k = jax.random.split(base, 2)
    shape_k = (SECTIONS, TOKENS, KV, HD)
    shape_q = (SECTIONS, TOKENS, HQ, HD)
    keys_out = jnp.clip(jax.random.normal(key_k, shape_k, jnp.float32), -4.0, 4.0)
    queries_out = jnp.clip(jax.random.normal(key_q, shape_q, jnp.float32), -4.0, 4.0)
    return (queries_out.reshape(SECTIONS, TOKENS, HQ * HD), keys_out.reshape(SECTIONS, TOKENS, KV * HD))


def draw_queries(key, part):
    return query_key_pair(key)[0].astype(jnp.bfloat16)


def draw_key_rows(key, part):
    return query_key_pair(key)[1].astype(jnp.bfloat16)


def block_levels(rng, extent, cuts, low, high):
    def one(position, shards_of):
        heights = jax.random.uniform(jax.random.fold_in(jax.random.fold_in(rng, 6), position), (shards_of,), jnp.float32, low / len(cuts), high / len(cuts))
        return jnp.repeat(jnp.exp(heights), extent[position] // shards_of).reshape((-1,) + (1,) * (len(extent) - position - 1))

    factor_of = one(*cuts[0])
    for cut in cuts[1:]:
        factor_of = factor_of * one(*cut)
    return factor_of


def centred(rng, shape, deviation, reach, cuts=(), kind=jnp.bfloat16):
    loudness = block_levels(rng, shape, cuts, -0.22, 0.18) if cuts else 1.0
    values = jax.random.normal(rng, shape, jnp.float32) * deviation * loudness
    return jnp.minimum(jnp.maximum(values, -reach), reach).astype(kind)


def setup_inputs(seed: int = 0) -> dict:
    seeds = jax.random.split(jax.random.key(seed), 10)
    stretch_order = draw_stretch_order(jax.random.fold_in(seeds[9], 71), 0)
    queries = draw_queries(jax.random.fold_in(seeds[9], 71), 0)
    key_rows = draw_key_rows(jax.random.fold_in(seeds[9], 71), 0)
    value_rows = centred(seeds[3], (SECTIONS, TOKENS, KV * HD), 1.0, 5.0, ((0, 4), (1, 2), (2, 4)))
    out_grad = centred(seeds[4], (SECTIONS, TOKENS, D), 1.0, 6.0, ((0, 4), (1, 8)))
    query_weight = centred(seeds[5], (SECTIONS, D, HQ * HD), D ** -0.5, 0.09375, ((0, 4), (2, 4)))
    key_weight = centred(seeds[6], (SECTIONS, D, KV * HD), D ** -0.5, 0.09375, ((0, 4), (2, 4)))
    value_weight = centred(seeds[7], (SECTIONS, D, KV * HD), D ** -0.5, 0.09375, ((0, 4), (2, 4)))
    output_weight = centred(seeds[8], (SECTIONS, HQ * HD, D), (HQ * HD) ** -0.5, 0.125, ((0, 4), (1, 4)))
    return {"stretch_order": stretch_order, "queries": queries, "key_rows": key_rows, "value_rows": value_rows, "out_grad": out_grad, "query_weight": query_weight, "key_weight": key_weight, "value_weight": value_weight, "output_weight": output_weight}


def token_positions(stretch_order):
    block_len = TOK_DEV // 2
    row_ids = jnp.arange(N_CTX * TOK_DEV, dtype=jnp.int32)
    flat_order = stretch_order.reshape(-1).astype(jnp.int32)
    return flat_order[row_ids // block_len] * block_len + row_ids % block_len


def section_grads(visible, queries, key_rows, value_rows, out_grad, query_weight, key_weight, value_weight, output_weight):
    score_scale = HD ** -0.5
    group_len = HQ // KV
    attn_grad = jnp.dot(out_grad, output_weight.T, preferred_element_type=jnp.float32).astype(jnp.bfloat16)

    def per_group(kv_idx):
        keys_head = lax.dynamic_slice_in_dim(key_rows, (kv_idx * HD).astype(jnp.int32), HD, 1)
        values_head = lax.dynamic_slice_in_dim(value_rows, (kv_idx * HD).astype(jnp.int32), HD, 1)

        def per_head(head_idx):
            column = ((kv_idx * group_len + head_idx) * HD).astype(jnp.int32)
            query_head = lax.dynamic_slice_in_dim(queries, column, HD, 1)
            grad_head = lax.dynamic_slice_in_dim(attn_grad, column, HD, 1)
            scores = jnp.dot(query_head, keys_head.T, preferred_element_type=jnp.float32) * score_scale
            grad_probs = jnp.dot(grad_head, values_head.T, preferred_element_type=jnp.float32)
            masked = jnp.where(visible, scores, -jnp.inf)
            lse = jax.nn.logsumexp(masked, axis=1)
            probs = jnp.where(visible, jnp.exp(masked - lse[:, None]), 0.0)
            delta = jnp.sum(probs * grad_probs, axis=1)
            dscore = probs * (grad_probs - delta[:, None])
            probs_low = probs.astype(jnp.bfloat16)
            dscore_low = dscore.astype(jnp.bfloat16)
            query_part = jnp.dot(dscore_low, keys_head, preferred_element_type=jnp.float32) * score_scale
            key_part = jnp.dot(dscore_low.T, query_head, preferred_element_type=jnp.float32) * score_scale
            value_part = jnp.dot(probs_low.T, grad_head, preferred_element_type=jnp.float32)
            return query_part, key_part, value_part

        query_parts, key_parts, value_parts = lax.map(per_head, jnp.arange(group_len, dtype=jnp.int32))
        return query_parts, jnp.sum(key_parts, axis=0), jnp.sum(value_parts, axis=0)

    query_all, key_all, value_all = lax.map(per_group, jnp.arange(KV, dtype=jnp.int32))
    seq_len = queries.shape[0]
    query_grad = jnp.transpose(query_all, (2, 0, 1, 3)).reshape(seq_len, HQ * HD).astype(jnp.bfloat16)
    key_grad = jnp.transpose(key_all, (1, 0, 2)).reshape(seq_len, KV * HD).astype(jnp.bfloat16)
    value_grad = jnp.transpose(value_all, (1, 0, 2)).reshape(seq_len, KV * HD).astype(jnp.bfloat16)
    head_cols = HQ * HD // N_TP
    kv_cols = KV * HD // N_TP
    summed = jnp.zeros((seq_len, D), jnp.float32)
    for member in range(N_TP):
        qa, qb = member * head_cols, (member + 1) * head_cols
        ka, kb = member * kv_cols, (member + 1) * kv_cols
        term = jnp.dot(query_grad[:, qa:qb], query_weight[:, qa:qb].T, preferred_element_type=jnp.float32)
        term = term + jnp.dot(key_grad[:, ka:kb], key_weight[:, ka:kb].T, preferred_element_type=jnp.float32)
        term = term + jnp.dot(value_grad[:, ka:kb], value_weight[:, ka:kb].T, preferred_element_type=jnp.float32)
        rounded = lax.optimization_barrier(term.astype(jnp.bfloat16))
        summed = summed + rounded.astype(jnp.float32)
    return summed.astype(jnp.bfloat16), key_grad, value_grad


def reference(stretch_order, queries, key_rows, value_rows, out_grad, query_weight, key_weight, value_weight, output_weight):
    positions = token_positions(stretch_order)
    visible = positions[None, :] <= positions[:, None]
    input_list = []
    key_list = []
    value_list = []
    for section_idx in range(SECTIONS):
        input_grad, key_grad, value_grad = section_grads(visible, queries[section_idx], key_rows[section_idx], value_rows[section_idx], out_grad[section_idx], query_weight[section_idx], key_weight[section_idx], value_weight[section_idx], output_weight[section_idx])
        input_list.append(input_grad)
        key_list.append(key_grad)
        value_list.append(value_grad)
    sent_grad = jnp.roll(jnp.stack(input_list), -1, axis=0)
    return sent_grad, jnp.stack(key_list), jnp.stack(value_list)
```

```python
import functools

import jax
import jax.numpy as jnp
from jax import lax
from jax.experimental import pallas as pl
from jax.experimental.pallas import tpu as pltpu
from jax.sharding import PartitionSpec as P

HD = 128
BLOCK = 256
MASKED = -1e30
LOG2E = 1.4426950408889634
CHUNK = 512
MESH = pl.DeviceIdType.MESH
VMEM = pl.BlockSpec(memory_space=pltpu.VMEM)
SMEM = pl.BlockSpec(memory_space=pltpu.SMEM)
LIMIT = 56 * 1024 * 1024


def dot_nt(lhs, rhs):
    return lax.dot_general(lhs, rhs, (((1,), (1,)), ((), ())), preferred_element_type=jnp.float32)


def dot_nn(lhs, rhs):
    return jnp.dot(lhs, rhs, preferred_element_type=jnp.float32)


def greet(peers):
    barrier = pltpu.get_barrier_semaphore()
    for peer in peers:
        pl.semaphore_signal(barrier, inc=1, device_id=peer, device_id_type=MESH)
    pl.semaphore_wait(barrier, len(peers))


def gather_kernel(
    n_tp, n_ctx, og_ref, wo_ref, k_ref, v_ref, grad_ref, kall_ref, vall_ref,
    shards, og_send, og_recv, kv_send, kv_recv,
):
    me = lax.axis_index("tp")
    ctx = lax.axis_index("ctx")
    rows = og_ref.shape[0]
    tok = k_ref.shape[0]
    greet(
        [{"tp": lax.rem(me + i, n_tp)} for i in range(1, n_tp)]
        + [{"ctx": lax.rem(ctx + i, n_ctx)} for i in range(1, n_ctx)]
    )
    sent = []
    for i in range(1, n_tp):
        copy = pltpu.make_async_remote_copy(
            src_ref=og_ref, dst_ref=shards.at[i - 1], send_sem=og_send.at[i - 1],
            recv_sem=og_recv.at[i - 1], device_id={"tp": lax.rem(me + i, n_tp)},
            device_id_type=MESH,
        )
        copy.start()
        sent.append(copy)
    place = pl.ds(pl.multiple_of(ctx * tok, tok), tok)
    kv_sent = []
    for i in range(1, n_ctx):
        for which, (src, dst) in enumerate(((k_ref, kall_ref), (v_ref, vall_ref))):
            copy = pltpu.make_async_remote_copy(
                src_ref=src, dst_ref=dst.at[place], send_sem=kv_send.at[which, i - 1],
                recv_sem=kv_recv.at[which, i - 1], device_id={"ctx": lax.rem(ctx + i, n_ctx)},
                device_id_type=MESH,
            )
            copy.start()
            kv_sent.append(copy)
    kall_ref[place, :] = k_ref[...]
    vall_ref[place, :] = v_ref[...]

    def store(owner, block):
        at = pl.ds(pl.multiple_of(owner * rows, rows), rows)
        grad_ref[at, :] = dot_nt(block[...], wo_ref[...]).astype(grad_ref.dtype)

    store(me, og_ref)
    for i in range(1, n_tp):
        sent[i - 1].wait_recv()
        store(lax.rem(me - i + n_tp, n_tp), shards.at[i - 1])
    for i in range(1, n_ctx):
        source = lax.rem(ctx - i + n_ctx, n_ctx)
        at = pl.ds(pl.multiple_of(source * tok, tok), tok)
        for which, (src, dst) in enumerate(((k_ref, kall_ref), (v_ref, vall_ref))):
            pltpu.make_async_remote_copy(
                src_ref=src, dst_ref=dst.at[at], send_sem=kv_send.at[which, i - 1],
                recv_sem=kv_recv.at[which, i - 1], device_id={"ctx": lax.rem(ctx + i, n_ctx)},
                device_id_type=MESH,
            ).wait_recv()
    for copy in sent + kv_sent:
        copy.wait_send()


def attention_kernel(
    order_ref, q_ref, g_ref, k_ref, v_ref, dq_ref, dkv_ref, dk_acc, dv_acc, kt_ref
):
    ctx = lax.axis_index("ctx")
    blocks = k_ref.shape[0] // BLOCK
    heads = q_ref.shape[1] // HD
    scale = HD ** (-0.5)
    for b in range(blocks):
        at = slice(b * BLOCK, (b + 1) * BLOCK)
        kt_ref[:, at] = k_ref[at, :].astype(jnp.float32).T.astype(jnp.bfloat16)
    dk_acc[...] = jnp.zeros_like(dk_acc)
    dv_acc[...] = jnp.zeros_like(dv_acc)
    shape = (BLOCK, BLOCK)
    lead = lax.broadcasted_iota(jnp.int32, shape, 0) - lax.broadcasted_iota(jnp.int32, shape, 1)

    def step(i, _):
        half, head = i // heads, lax.rem(i, heads)
        rows = pl.ds(pl.multiple_of(half * BLOCK, BLOCK), BLOCK)
        cols = pl.ds(pl.multiple_of(head * HD, HD), HD)
        q = q_ref[rows, cols]
        g = g_ref[rows, cols]
        query_id = order_ref[ctx, half]
        scores = []
        for b in range(blocks):
            ahead = (query_id - order_ref[b // 2, b % 2]) * BLOCK
            s = dot_nt(k_ref[b * BLOCK:(b + 1) * BLOCK, :], q)
            scores.append(jnp.where(lead <= ahead, s, MASKED))
        top = functools.reduce(
            jnp.maximum, [jnp.max(s, axis=0, keepdims=True) for s in scores]
        )
        weights = [jnp.exp2((s - top) * (scale * LOG2E)) for s in scores]
        gps = [dot_nt(v_ref[b * BLOCK:(b + 1) * BLOCK, :], g) for b in range(blocks)]
        total = sum(jnp.sum(w, axis=0, keepdims=True) for w in weights)
        dots = sum(jnp.sum(w * p, axis=0, keepdims=True) for w, p in zip(weights, gps))
        inv = 1.0 / total
        delta = dots * inv
        dqt = jnp.zeros((HD, BLOCK), jnp.float32)
        for b in range(blocks):
            at = slice(b * BLOCK, (b + 1) * BLOCK)
            probs = weights[b] * inv
            ds = (probs * (gps[b] - delta)).astype(jnp.bfloat16)
            dv_acc[at, :] += dot_nn(probs.astype(jnp.bfloat16), g)
            dk_acc[at, :] += dot_nn(ds, q)
            dqt += dot_nn(kt_ref[:, at], ds)
        dq_ref[rows, cols] = (dqt * scale).T.astype(dq_ref.dtype)
        return 0

    lax.fori_loop(0, 2 * heads, step, 0)
    dkv_ref[0] = (dk_acc[...] * scale).astype(dkv_ref.dtype)
    dkv_ref[1] = dv_acc[...].astype(dkv_ref.dtype)


def scatter_kernel(
    n_tp, n_ctx, n_sec, dq_ref, dkv_ref, wq_ref, wk_ref, wv_ref, out_ref, kg_ref, vg_ref,
    parts, right_in, right_out, left_in, left_out, relay,
    part_send, part_recv, right_send, right_recv, left_send, left_recv, relay_send, relay_recv,
):
    me = lax.axis_index("tp")
    ctx = lax.axis_index("ctx")
    sec = lax.axis_index("section")
    tok = kg_ref.shape[0]
    rows = out_ref.shape[0]
    chunks = out_ref.shape[1] // CHUNK
    before = lax.rem(sec + n_sec - 1, n_sec)
    greet(
        [{"tp": lax.rem(me + i, n_tp)} for i in range(1, n_tp)]
        + [{"ctx": lax.rem(ctx + i, n_ctx)} for i in range(1, n_ctx)]
        + [{"section": before}, {"section": lax.rem(sec + 1, n_sec)}]
    )
    part_sent = []
    for i in range(1, n_ctx):
        peer = lax.rem(ctx + i, n_ctx)
        copy = pltpu.make_async_remote_copy(
            src_ref=dkv_ref.at[:, pl.ds(pl.multiple_of(peer * tok, tok), tok)],
            dst_ref=parts.at[i - 1], send_sem=part_send.at[i - 1],
            recv_sem=part_recv.at[i - 1], device_id={"ctx": peer}, device_id_type=MESH,
        )
        copy.start()
        part_sent.append(copy)
    mine = pl.ds(pl.multiple_of(ctx * tok, tok), tok)
    kg = dkv_ref[0, mine, :].astype(jnp.float32)
    vg = dkv_ref[1, mine, :].astype(jnp.float32)
    for i in range(1, n_ctx):
        part_sent[i - 1].wait_recv()
        kg += parts[i - 1, 0].astype(jnp.float32)
        vg += parts[i - 1, 1].astype(jnp.float32)
    kg_ref[...] = kg.astype(kg_ref.dtype)
    vg_ref[...] = vg.astype(vg_ref.dtype)

    def term(block, c):
        at = pl.ds(pl.multiple_of(block * rows, rows), rows)
        cols = pl.ds(pl.multiple_of(c * CHUNK, CHUNK), CHUNK)
        out = dot_nt(dq_ref[at, :], wq_ref[cols, :])
        out += dot_nt(kg_ref[at, :], wk_ref[cols, :])
        out += dot_nt(vg_ref[at, :], wv_ref[cols, :])
        return out

    def right_copy(block, c):
        return pltpu.make_async_remote_copy(
            src_ref=right_out.at[block, c], dst_ref=right_in.at[block, c],
            send_sem=right_send.at[block, c], recv_sem=right_recv.at[block, c],
            device_id={"tp": lax.rem(me + 1, n_tp)}, device_id_type=MESH,
        )

    def left_copy(block, c):
        return pltpu.make_async_remote_copy(
            src_ref=left_out.at[block, c], dst_ref=left_in.at[block, c],
            send_sem=left_send.at[block, c], recv_sem=left_recv.at[block, c],
            device_id={"tp": lax.rem(me + n_tp - 1, n_tp)}, device_id_type=MESH,
        )

    def relay_copy(c):
        cols = pl.ds(pl.multiple_of(c * CHUNK, CHUNK), CHUNK)
        return pltpu.make_async_remote_copy(
            src_ref=relay.at[c], dst_ref=out_ref.at[:, cols],
            send_sem=relay_send.at[c], recv_sem=relay_recv.at[c],
            device_id={"section": before}, device_id_type=MESH,
        )

    def forward(make, inbox, outbox, has_source, block, c):
        outbox[block, c] = term(block, c).astype(outbox.dtype)

        @pl.when(has_source)
        def _():
            make(block, c).wait_recv()
            outbox[block, c] = (
                outbox[block, c].astype(jnp.float32) + inbox[block, c].astype(jnp.float32)
            ).astype(outbox.dtype)

        make(block, c).start()

    def forward_step(i, _):
        turn, c = i // chunks, lax.rem(i, chunks)
        far = n_tp - 1 - turn

        @pl.when(far > me)
        def _():
            forward(right_copy, right_in, right_out, me > 0, far, c)

        @pl.when(turn < me)
        def _():
            forward(left_copy, left_in, left_out, me < n_tp - 1, turn, c)

        return 0

    lax.fori_loop(0, (n_tp - 1) * chunks, forward_step, 0)

    def final_step(c, _):
        relay[c] = term(me, c).astype(relay.dtype)

        @pl.when(me > 0)
        def _():
            right_copy(me, c).wait_recv()
            relay[c] = (
                relay[c].astype(jnp.float32) + right_in[me, c].astype(jnp.float32)
            ).astype(relay.dtype)

        @pl.when(me < n_tp - 1)
        def _():
            left_copy(me, c).wait_recv()
            relay[c] = (
                relay[c].astype(jnp.float32) + left_in[me, c].astype(jnp.float32)
            ).astype(relay.dtype)

        relay_copy(c).start()
        return 0

    lax.fori_loop(0, chunks, final_step, 0)

    def drain_step(i, _):
        turn, c = i // chunks, lax.rem(i, chunks)
        far = n_tp - 1 - turn

        @pl.when(far > me)
        def _():
            right_copy(far, c).wait_send()

        @pl.when(turn < me)
        def _():
            left_copy(turn, c).wait_send()

        return 0

    lax.fori_loop(0, (n_tp - 1) * chunks, drain_step, 0)

    def relay_step(c, _):
        relay_copy(c).wait_send()
        relay_copy(c).wait_recv()
        return 0

    lax.fori_loop(0, chunks, relay_step, 0)
    for copy in part_sent:
        copy.wait_send()


def per_device(
    n_tp, n_ctx, n_sec, stretch_order, queries, key_rows, value_rows, out_grad,
    query_weight, key_weight, value_weight, output_weight,
):
    tok, q_cols = queries.shape[1:]
    rows, width = out_grad.shape[1:]
    seq = tok * n_ctx
    low = jnp.bfloat16
    dma = pltpu.SemaphoreType.DMA
    chunks = width // CHUNK
    attn_grad, keys_all, values_all = pl.pallas_call(
        functools.partial(gather_kernel, n_tp, n_ctx),
        out_shape=(
            jax.ShapeDtypeStruct((tok, q_cols), low),
            jax.ShapeDtypeStruct((seq, HD), low),
            jax.ShapeDtypeStruct((seq, HD), low),
        ),
        in_specs=[VMEM] * 4,
        out_specs=(VMEM,) * 3,
        scratch_shapes=[
            pltpu.VMEM((n_tp - 1, rows, width), low),
            dma((n_tp - 1,)), dma((n_tp - 1,)),
            dma((2, n_ctx - 1)), dma((2, n_ctx - 1)),
        ],
        compiler_params=pltpu.CompilerParams(
            collective_id=0, has_side_effects=True, vmem_limit_bytes=LIMIT
        ),
    )(out_grad[0], output_weight[0], key_rows[0], value_rows[0])
    query_grad, kv_parts = pl.pallas_call(
        attention_kernel,
        out_shape=(
            jax.ShapeDtypeStruct((tok, q_cols), low),
            jax.ShapeDtypeStruct((2, seq, HD), low),
        ),
        in_specs=[SMEM] + [VMEM] * 4,
        out_specs=(VMEM,) * 2,
        scratch_shapes=[
            pltpu.VMEM((seq, HD), jnp.float32),
            pltpu.VMEM((seq, HD), jnp.float32),
            pltpu.VMEM((HD, seq), low),
        ],
        compiler_params=pltpu.CompilerParams(vmem_limit_bytes=LIMIT),
    )(stretch_order, queries[0], attn_grad, keys_all, values_all)
    travel = pltpu.VMEM((n_tp, chunks, rows, CHUNK), low)
    sent_grad, key_grad, value_grad = pl.pallas_call(
        functools.partial(scatter_kernel, n_tp, n_ctx, n_sec),
        out_shape=(
            jax.ShapeDtypeStruct((rows, width), low),
            jax.ShapeDtypeStruct((tok, HD), low),
            jax.ShapeDtypeStruct((tok, HD), low),
        ),
        in_specs=[VMEM] * 5,
        out_specs=(VMEM,) * 3,
        scratch_shapes=[
            pltpu.VMEM((n_ctx - 1, 2, tok, HD), low),
            travel, travel, travel, travel,
            pltpu.VMEM((chunks, rows, CHUNK), low),
            dma((n_ctx - 1,)), dma((n_ctx - 1,)),
            dma((n_tp, chunks)), dma((n_tp, chunks)),
            dma((n_tp, chunks)), dma((n_tp, chunks)),
            dma((chunks,)), dma((chunks,)),
        ],
        compiler_params=pltpu.CompilerParams(
            collective_id=1, has_side_effects=True, vmem_limit_bytes=LIMIT
        ),
    )(query_grad, kv_parts, query_weight[0], key_weight[0], value_weight[0])
    return (sent_grad[None], key_grad[None], value_grad[None])


def solution(mesh):
    placed = (
        P(),
        P("section", "ctx", "tp"),
        P("section", "ctx", "tp"),
        P("section", "ctx", "tp"),
        P("section", ("ctx", "tp"), None),
        P("section", None, "tp"),
        P("section", None, "tp"),
        P("section", None, "tp"),
        P("section", "tp", None),
    )
    body = functools.partial(
        per_device, mesh.shape["tp"], mesh.shape["ctx"], mesh.shape["section"]
    )
    return jax.shard_map(
        body,
        mesh=mesh,
        in_specs=placed,
        out_specs=(
            P("section", ("ctx", "tp"), None),
            P("section", "ctx", "tp"),
            P("section", "ctx", "tp"),
        ),
        check_vma=False,
    )
```

```python
import functools

import jax
import jax.numpy as jnp
from jax import lax
from jax.experimental import pallas as pl
from jax.experimental.pallas import tpu as pltpu
from jax.sharding import PartitionSpec as P

HD = 128
BLOCK = 256
MASKED = -1e30
LOG2E = 1.4426950408889634
CHUNK = 512
PIECE = 32
LAG = 3
MESH = pl.DeviceIdType.MESH
VMEM = pl.BlockSpec(memory_space=pltpu.VMEM)
SMEM = pl.BlockSpec(memory_space=pltpu.SMEM)
LIMIT = 56 * 1024 * 1024


def dot_nt(lhs, rhs):
    return lax.dot_general(lhs, rhs, (((1,), (1,)), ((), ())), preferred_element_type=jnp.float32)


def dot_nn(lhs, rhs):
    return jnp.dot(lhs, rhs, preferred_element_type=jnp.float32)


def greet(peers):
    barrier = pltpu.get_barrier_semaphore()
    for peer in peers:
        pl.semaphore_signal(barrier, inc=1, device_id=peer, device_id_type=MESH)
    pl.semaphore_wait(barrier, len(peers))


def gather_kernel(
    n_tp, n_ctx, og_ref, wo_ref, k_ref, v_ref, grad_ref, kall_ref, vall_ref,
    shards, og_send, og_recv, kv_send, kv_recv,
):
    me = lax.axis_index("tp")
    ctx = lax.axis_index("ctx")
    rows = og_ref.shape[0]
    tok = k_ref.shape[0]
    greet(
        [{"tp": lax.rem(me + i, n_tp)} for i in range(1, n_tp)]
        + [{"ctx": lax.rem(ctx + i, n_ctx)} for i in range(1, n_ctx)]
    )
    pieces = rows // PIECE

    def hop(which, owner, c, own):
        at = pl.ds(pl.multiple_of(c * PIECE, PIECE), PIECE)
        step = n_tp - 1 if which else 1
        return pltpu.make_async_remote_copy(
            src_ref=og_ref.at[at] if own else shards.at[owner, at],
            dst_ref=shards.at[owner, at], send_sem=og_send.at[which, owner, c],
            recv_sem=og_recv.at[which, owner, c],
            device_id={"tp": lax.rem(me + step, n_tp)}, device_id_type=MESH,
        )

    def own_step(c, _):
        @pl.when(me < n_tp - 1)
        def _():
            hop(0, me, c, True).start()

        @pl.when(me > 0)
        def _():
            hop(1, me, c, True).start()

        return 0

    place = pl.ds(pl.multiple_of(ctx * tok, tok), tok)
    kv_sent = []
    for i in range(1, n_ctx):
        for which, (src, dst) in enumerate(((k_ref, kall_ref), (v_ref, vall_ref))):
            copy = pltpu.make_async_remote_copy(
                src_ref=src, dst_ref=dst.at[place], send_sem=kv_send.at[which, i - 1],
                recv_sem=kv_recv.at[which, i - 1], device_id={"ctx": lax.rem(ctx + i, n_ctx)},
                device_id_type=MESH,
            )
            copy.start()
            kv_sent.append(copy)
    lax.fori_loop(0, pieces, own_step, 0)
    kall_ref[place, :] = k_ref[...]
    vall_ref[place, :] = v_ref[...]

    def store(owner, block):
        at = pl.ds(pl.multiple_of(owner * rows, rows), rows)
        grad_ref[at, :] = dot_nt(block[...], wo_ref[...]).astype(grad_ref.dtype)

    store(me, og_ref)
    for d in range(1, n_tp):
        def pass_on(c, _):
            @pl.when(me >= d)
            def _():
                hop(0, me - d, c, False).wait_recv()

                @pl.when(me < n_tp - 1)
                def _():
                    hop(0, me - d, c, False).start()

            @pl.when(me + d < n_tp)
            def _():
                hop(1, me + d, c, False).wait_recv()

                @pl.when(me > 0)
                def _():
                    hop(1, me + d, c, False).start()

            return 0

        lax.fori_loop(0, pieces, pass_on, 0)

        @pl.when(me >= d)
        def _():
            store(me - d, shards.at[me - d])

        @pl.when(me + d < n_tp)
        def _():
            store(me + d, shards.at[me + d])

    for i in range(1, n_ctx):
        source = lax.rem(ctx - i + n_ctx, n_ctx)
        at = pl.ds(pl.multiple_of(source * tok, tok), tok)
        for which, (src, dst) in enumerate(((k_ref, kall_ref), (v_ref, vall_ref))):
            pltpu.make_async_remote_copy(
                src_ref=src, dst_ref=dst.at[at], send_sem=kv_send.at[which, i - 1],
                recv_sem=kv_recv.at[which, i - 1], device_id={"ctx": lax.rem(ctx + i, n_ctx)},
                device_id_type=MESH,
            ).wait_recv()
    for copy in kv_sent:
        copy.wait_send()

    def drained(i, _):
        owner, c = i // pieces, lax.rem(i, pieces)

        @pl.when((owner <= me) & (me < n_tp - 1))
        def _():
            hop(0, owner, c, False).wait_send()

        @pl.when((owner >= me) & (me > 0))
        def _():
            hop(1, owner, c, False).wait_send()

        return 0

    lax.fori_loop(0, n_tp * pieces, drained, 0)


def attention_kernel(
    order_ref, q_ref, g_ref, k_ref, v_ref, dq_ref, dkv_ref, dk_acc, dv_acc, kt_ref
):
    ctx = lax.axis_index("ctx")
    blocks = k_ref.shape[0] // BLOCK
    heads = q_ref.shape[1] // HD
    scale = HD ** (-0.5)
    for b in range(blocks):
        at = slice(b * BLOCK, (b + 1) * BLOCK)
        kt_ref[:, at] = k_ref[at, :].astype(jnp.float32).T.astype(jnp.bfloat16)
    dk_acc[...] = jnp.zeros_like(dk_acc)
    dv_acc[...] = jnp.zeros_like(dv_acc)
    shape = (BLOCK, BLOCK)
    lead = lax.broadcasted_iota(jnp.int32, shape, 0) - lax.broadcasted_iota(jnp.int32, shape, 1)

    def step(i, _):
        half, head = i // heads, lax.rem(i, heads)
        rows = pl.ds(pl.multiple_of(half * BLOCK, BLOCK), BLOCK)
        cols = pl.ds(pl.multiple_of(head * HD, HD), HD)
        q = q_ref[rows, cols]
        g = g_ref[rows, cols]
        query_id = order_ref[ctx, half]
        scores = []
        for b in range(blocks):
            ahead = (query_id - order_ref[b // 2, b % 2]) * BLOCK
            s = dot_nt(k_ref[b * BLOCK:(b + 1) * BLOCK, :], q)
            scores.append(jnp.where(lead <= ahead, s, MASKED))
        top = functools.reduce(
            jnp.maximum, [jnp.max(s, axis=0, keepdims=True) for s in scores]
        )
        weights = [jnp.exp2((s - top) * (scale * LOG2E)) for s in scores]
        gps = [dot_nt(v_ref[b * BLOCK:(b + 1) * BLOCK, :], g) for b in range(blocks)]
        total = sum(jnp.sum(w, axis=0, keepdims=True) for w in weights)
        dots = sum(jnp.sum(w * p, axis=0, keepdims=True) for w, p in zip(weights, gps))
        inv = 1.0 / total
        delta = dots * inv
        dqt = jnp.zeros((HD, BLOCK), jnp.float32)
        for b in range(blocks):
            at = slice(b * BLOCK, (b + 1) * BLOCK)
            probs = weights[b] * inv
            ds = (probs * (gps[b] - delta)).astype(jnp.bfloat16)
            dv_acc[at, :] += dot_nn(probs.astype(jnp.bfloat16), g)
            dk_acc[at, :] += dot_nn(ds, q)
            dqt += dot_nn(kt_ref[:, at], ds)
        dq_ref[rows, cols] = (dqt * scale).T.astype(dq_ref.dtype)
        return 0

    lax.fori_loop(0, 2 * heads, step, 0)
    dkv_ref[0] = (dk_acc[...] * scale).astype(dkv_ref.dtype)
    dkv_ref[1] = dv_acc[...].astype(dkv_ref.dtype)


def scatter_kernel(
    n_tp, n_ctx, n_sec, dq_ref, dkv_ref, wq_ref, wk_ref, wv_ref, out_ref, kg_ref, vg_ref,
    parts, right_in, right_out, left_in, left_out, relay,
    part_send, part_recv, right_send, right_recv, left_send, left_recv, relay_send, relay_recv,
):
    me = lax.axis_index("tp")
    ctx = lax.axis_index("ctx")
    sec = lax.axis_index("section")
    tok = kg_ref.shape[0]
    rows = out_ref.shape[0]
    chunks = out_ref.shape[1] // CHUNK
    before = lax.rem(sec + n_sec - 1, n_sec)
    greet(
        [{"tp": lax.rem(me + i, n_tp)} for i in range(1, n_tp)]
        + [{"ctx": lax.rem(ctx + i, n_ctx)} for i in range(1, n_ctx)]
        + [{"section": before}, {"section": lax.rem(sec + 1, n_sec)}]
    )
    part_sent = []
    for i in range(1, n_ctx):
        peer = lax.rem(ctx + i, n_ctx)
        copy = pltpu.make_async_remote_copy(
            src_ref=dkv_ref.at[:, pl.ds(pl.multiple_of(peer * tok, tok), tok)],
            dst_ref=parts.at[i - 1], send_sem=part_send.at[i - 1],
            recv_sem=part_recv.at[i - 1], device_id={"ctx": peer}, device_id_type=MESH,
        )
        copy.start()
        part_sent.append(copy)
    mine = pl.ds(pl.multiple_of(ctx * tok, tok), tok)
    kg = dkv_ref[0, mine, :].astype(jnp.float32)
    vg = dkv_ref[1, mine, :].astype(jnp.float32)
    for i in range(1, n_ctx):
        part_sent[i - 1].wait_recv()
        kg += parts[i - 1, 0].astype(jnp.float32)
        vg += parts[i - 1, 1].astype(jnp.float32)
    kg_ref[...] = kg.astype(kg_ref.dtype)
    vg_ref[...] = vg.astype(vg_ref.dtype)

    def term(block, c):
        at = pl.ds(pl.multiple_of(block * rows, rows), rows)
        cols = pl.ds(pl.multiple_of(c * CHUNK, CHUNK), CHUNK)
        out = dot_nt(dq_ref[at, :], wq_ref[cols, :])
        out += dot_nt(kg_ref[at, :], wk_ref[cols, :])
        out += dot_nt(vg_ref[at, :], wv_ref[cols, :])
        return out

    def right_copy(block, c):
        return pltpu.make_async_remote_copy(
            src_ref=right_out.at[block, c], dst_ref=right_in.at[block, c],
            send_sem=right_send.at[block, c], recv_sem=right_recv.at[block, c],
            device_id={"tp": lax.rem(me + 1, n_tp)}, device_id_type=MESH,
        )

    def left_copy(block, c):
        return pltpu.make_async_remote_copy(
            src_ref=left_out.at[block, c], dst_ref=left_in.at[block, c],
            send_sem=left_send.at[block, c], recv_sem=left_recv.at[block, c],
            device_id={"tp": lax.rem(me + n_tp - 1, n_tp)}, device_id_type=MESH,
        )

    def relay_copy(c):
        cols = pl.ds(pl.multiple_of(c * CHUNK, CHUNK), CHUNK)
        return pltpu.make_async_remote_copy(
            src_ref=relay.at[c], dst_ref=out_ref.at[:, cols],
            send_sem=relay_send.at[c], recv_sem=relay_recv.at[c],
            device_id={"section": before}, device_id_type=MESH,
        )

    def forward(make, inbox, outbox, has_source, block, c):
        outbox[block, c] = term(block, c).astype(outbox.dtype)

        @pl.when(has_source)
        def _():
            make(block, c).wait_recv()
            outbox[block, c] = (
                outbox[block, c].astype(jnp.float32) + inbox[block, c].astype(jnp.float32)
            ).astype(outbox.dtype)

        make(block, c).start()

    right_total = (n_tp - 1 - me) * chunks
    left_total = me * chunks
    left_lag = jnp.where(2 * me < n_tp, LAG, 0)
    right_lag = LAG - left_lag

    def forward_step(i, _):
        r = i - right_lag
        l = i - left_lag

        @pl.when((2 * me < n_tp) & (r < right_total))
        def _():
            forward(right_copy, right_in, right_out, me > 0, n_tp - 1 - r // chunks, lax.rem(r, chunks))

        @pl.when((l >= 0) & (l < left_total))
        def _():
            forward(left_copy, left_in, left_out, me < n_tp - 1, l // chunks, lax.rem(l, chunks))

        @pl.when((2 * me >= n_tp) & (r >= 0) & (r < right_total))
        def _():
            forward(right_copy, right_in, right_out, me > 0, n_tp - 1 - r // chunks, lax.rem(r, chunks))

        return 0

    lax.fori_loop(0, (n_tp - 1) * chunks + LAG, forward_step, 0)

    def final_step(c, _):
        relay[c] = term(me, c).astype(relay.dtype)

        @pl.when(me > 0)
        def _():
            right_copy(me, c).wait_recv()
            relay[c] = (
                relay[c].astype(jnp.float32) + right_in[me, c].astype(jnp.float32)
            ).astype(relay.dtype)

        @pl.when(me < n_tp - 1)
        def _():
            left_copy(me, c).wait_recv()
            relay[c] = (
                relay[c].astype(jnp.float32) + left_in[me, c].astype(jnp.float32)
            ).astype(relay.dtype)

        relay_copy(c).start()
        return 0

    lax.fori_loop(0, chunks, final_step, 0)

    def drain_step(i, _):
        turn, c = i // chunks, lax.rem(i, chunks)
        far = n_tp - 1 - turn

        @pl.when(far > me)
        def _():
            right_copy(far, c).wait_send()

        @pl.when(turn < me)
        def _():
            left_copy(turn, c).wait_send()

        return 0

    lax.fori_loop(0, (n_tp - 1) * chunks, drain_step, 0)

    def relay_step(c, _):
        relay_copy(c).wait_send()
        relay_copy(c).wait_recv()
        return 0

    lax.fori_loop(0, chunks, relay_step, 0)
    for copy in part_sent:
        copy.wait_send()


def per_device(
    n_tp, n_ctx, n_sec, stretch_order, queries, key_rows, value_rows, out_grad,
    query_weight, key_weight, value_weight, output_weight,
):
    tok, q_cols = queries.shape[1:]
    rows, width = out_grad.shape[1:]
    seq = tok * n_ctx
    low = jnp.bfloat16
    dma = pltpu.SemaphoreType.DMA
    chunks = width // CHUNK
    attn_grad, keys_all, values_all = pl.pallas_call(
        functools.partial(gather_kernel, n_tp, n_ctx),
        out_shape=(
            jax.ShapeDtypeStruct((tok, q_cols), low),
            jax.ShapeDtypeStruct((seq, HD), low),
            jax.ShapeDtypeStruct((seq, HD), low),
        ),
        in_specs=[VMEM] * 4,
        out_specs=(VMEM,) * 3,
        scratch_shapes=[
            pltpu.VMEM((n_tp, rows, width), low),
            dma((2, n_tp, rows // PIECE)), dma((2, n_tp, rows // PIECE)),
            dma((2, n_ctx - 1)), dma((2, n_ctx - 1)),
        ],
        compiler_params=pltpu.CompilerParams(
            collective_id=0, has_side_effects=True, vmem_limit_bytes=LIMIT
        ),
    )(out_grad[0], output_weight[0], key_rows[0], value_rows[0])
    query_grad, kv_parts = pl.pallas_call(
        attention_kernel,
        out_shape=(
            jax.ShapeDtypeStruct((tok, q_cols), low),
            jax.ShapeDtypeStruct((2, seq, HD), low),
        ),
        in_specs=[SMEM] + [VMEM] * 4,
        out_specs=(VMEM,) * 2,
        scratch_shapes=[
            pltpu.VMEM((seq, HD), jnp.float32),
            pltpu.VMEM((seq, HD), jnp.float32),
            pltpu.VMEM((HD, seq), low),
        ],
        compiler_params=pltpu.CompilerParams(vmem_limit_bytes=LIMIT),
    )(stretch_order, queries[0], attn_grad, keys_all, values_all)
    travel = pltpu.VMEM((n_tp, chunks, rows, CHUNK), low)
    sent_grad, key_grad, value_grad = pl.pallas_call(
        functools.partial(scatter_kernel, n_tp, n_ctx, n_sec),
        out_shape=(
            jax.ShapeDtypeStruct((rows, width), low),
            jax.ShapeDtypeStruct((tok, HD), low),
            jax.ShapeDtypeStruct((tok, HD), low),
        ),
        in_specs=[VMEM] * 5,
        out_specs=(VMEM,) * 3,
        scratch_shapes=[
            pltpu.VMEM((n_ctx - 1, 2, tok, HD), low),
            travel, travel, travel, travel,
            pltpu.VMEM((chunks, rows, CHUNK), low),
            dma((n_ctx - 1,)), dma((n_ctx - 1,)),
            dma((n_tp, chunks)), dma((n_tp, chunks)),
            dma((n_tp, chunks)), dma((n_tp, chunks)),
            dma((chunks,)), dma((chunks,)),
        ],
        compiler_params=pltpu.CompilerParams(
            collective_id=1, has_side_effects=True, vmem_limit_bytes=LIMIT
        ),
    )(query_grad, kv_parts, query_weight[0], key_weight[0], value_weight[0])
    return (sent_grad[None], key_grad[None], value_grad[None])


def solution(mesh):
    placed = (
        P(),
        P("section", "ctx", "tp"),
        P("section", "ctx", "tp"),
        P("section", "ctx", "tp"),
        P("section", ("ctx", "tp"), None),
        P("section", None, "tp"),
        P("section", None, "tp"),
        P("section", None, "tp"),
        P("section", "tp", None),
    )
    body = functools.partial(
        per_device, mesh.shape["tp"], mesh.shape["ctx"], mesh.shape["section"]
    )
    return jax.shard_map(
        body,
        mesh=mesh,
        in_specs=placed,
        out_specs=(
            P("section", ("ctx", "tp"), None),
            P("section", "ctx", "tp"),
            P("section", "ctx", "tp"),
        ),
        check_vma=False,
    )
```
